32 devices in a mesh: slab: 4 (over z), half: 2 (over core), img: 4 (over y, x).
Axes of the slice: x: 2, y: 2, z: 4, core: 2. Of those that a mesh axis runs over, the one named last changes fastest.
Arguments:
- samples: bfloat16 [2048, 2, 96, 128], P(('half', 'slab', 'img')), parts along dimension 0, may hold values from -6 to 6
- kernels: bfloat16 [64, 128, 128], replicated, may hold values from -0.5 to 0.5
- dest: int32 [2048, 1], P(('half', 'slab', 'img')), parts along dimension 0, may hold values from 0 to 3; in each aligned block of 64 rows (0 to 63, 64 to 127, ...) at most 32 rows name the same one
- plane_off: int32 [2048], P(('half', 'slab', 'img')), parts along dimension 0, may hold values from 0 to 127
- kernel_id: int32 [2048], P(('half', 'slab', 'img')), parts along dimension 0, may hold values from 0 to 63
Outputs:
- volume: float32 [2, 192, 512, 512], P(None, ('half', 'img'), 'slab'), parts along dimension 1
The draws below stay inside these ranges and needn't reach their ends.
There are 2 independent parts, one for each index of `half`. The reference program is written for one: setup_inputs(seed, part) draws one part's arguments, and reference() takes and returns one part's arrays. A program takes and returns all parts, laid end to end along the dimension named above; an argument that names none is the same for every part. Nothing has to cross between parts.
Inputs may be any that keep to these rules, and one draw needn't show every extreme that they name: `dest`: in each aligned block of 64 rows (the slice blocks of one device) no slab is named by more than 32 rows.
All inputs are finite; a program needn't handle non-finite values.
Results may differ from the reference program's by a relative error of at most 0.0003.
Values may be sent and summed in bfloat16 or wider, within the bound.
A program may use at most 128 MiB of HBM per device.

```python
import math
import jax
import jax.numpy as jnp
import numpy as np
from jax import lax

NY = 512
NZ = 512
KW = 128
NK = 64
XW = 96
NB = 4
ITEMS_DEV = 64
ITEMS = 1024
ZL = 128
CAP = 32
N_SLAB = 4


def plant(values, key, low, top_value):
    place = [jax.random.randint(jax.random.fold_in(key, axis), (), 0, length) for axis, length in enumerate(values.shape)]
    longest = values.shape.index(max(values.shape))
    neighbour = place[:longest] + [(place[longest] + 1) % values.shape[longest]] + place[longest + 1:]
    return values.at[tuple(place)].set(low).at[tuple(neighbour)].set(top_value)


def block_scale(stream_key, extent, cuts, smallest, largest):
    factor_of, own = 1.0, jax.random.fold_in(stream_key, 6)
    for position, blocks in cuts:
        draws = jnp.exp(jax.random.uniform(jax.random.fold_in(own, position), (blocks,), jnp.float32, smallest / len(cuts), largest / len(cuts)))
        factor_of = factor_of * jnp.repeat(draws, extent[position] // blocks).reshape([-1 if axis == position else 1 for axis in range(len(extent))])
    return factor_of


def shared_out(own_key, own, number, rows, number_of, top, most, slope):
    order = jax.random.permutation(own_key, number_of)
    crowded, ordinary = portions_of(number_of, rows * top, most, slope, True), portions_of(number_of, rows * top, most, slope, False)
    places = jnp.arange(number_of)

    def named(lengths, offset_by):
        used = int((lengths > 0).sum())
        fixed = max(1, used // 4)
        passed = fixed + (places - fixed + offset_by * (used - fixed)) % max(1, number_of - fixed)
        return jnp.zeros((number_of,), jnp.int32).at[order[jnp.where(places < fixed, places, passed)]].set(jnp.asarray(lengths, jnp.int32))

    lengths = jnp.where(number % 4 == 0, named(crowded, number // 4), named(ordinary, number - number // 4 - 1))
    mixed = jax.random.permutation(jax.random.fold_in(own, 3), number_of)
    source_of, sink = mixed[0:number_of // 2 * 2:2], mixed[1:number_of // 2 * 2:2]
    slack = jnp.minimum(lengths[source_of] - 1, most - lengths[sink]) // 2
    slack = jnp.where((source_of == order[0]) | (sink == order[0]) | (lengths[sink] == 0), 0, jnp.maximum(slack, 0))
    passed = jax.random.randint(jax.random.fold_in(own, 4), (number_of // 2,), 0, 1 << 20) % (slack + 1)
    lengths = lengths.at[source_of].add(-passed).at[sink].add(passed)
    items = jnp.searchsorted(jnp.cumsum(lengths), jnp.arange(rows * top), side="right").astype(jnp.int32)
    table = items.reshape(top, rows).T
    table = table[jax.random.permutation(jax.random.fold_in(own, 1), rows)]
    offset_by = jax.random.randint(jax.random.fold_in(own, 2), (rows, 1), 0, top)
    return jnp.take_along_axis(table, (jnp.arange(top)[None, :] + offset_by) % top, axis=1)


def portions_of(count, total, most, skew, full):
    loads = [(1 << 20) // math.isqrt(grade ** skew) + 1 for grade in range(1, count + 1)]
    largest = most if full else min(most, max(-(-total // count), total * loads[0] // sum(loads)))
    least = 1 if total - largest >= count - 1 else 0
    given, rest = [largest] + [least] * (count - 1), total - largest - least * (count - 1)
    while rest > 0:
        free = [i for i in range(1, count) if given[i] < largest] or [i for i in range(1, count) if given[i] < most]
        pool, budget = sum([loads[i] for i in free]), rest
        for i in free:
            more = min(most - given[i], max(1, budget * loads[i] // pool), rest)
            given[i] = given[i] + more
            rest = rest - more
    return np.array(given)


def gaussian(stream_key, dims, width, most, split=(), held_as=jnp.bfloat16):
    array = jax.random.normal(stream_key, dims, jnp.float32) * width
    if len(split) > 0:
        array = block_scale(stream_key, dims, split, -0.22, 0.18) * array
    return jnp.clip(array, min=-most, max=most).astype(held_as)


def setup_inputs(seed: int = 0, part: int = 0) -> dict:
    seeds = jax.random.split(jax.random.key(seed), 6)
    part_keys = jax.random.split(jax.random.fold_in(seeds[5], part), 6)
    samples = gaussian(part_keys[0], (ITEMS, 2, XW, KW), 1.0, 6.0, ((0, 16),))
    kernels = gaussian(seeds[1], (NK, KW, KW), KW ** -0.5, 0.5)
    dest_keys = jax.random.split(jax.random.fold_in(part_keys[2], 1), ITEMS // ITEMS_DEV)
    dest_turns = jax.random.permutation(jax.random.fold_in(part_keys[2], 3), ITEMS // ITEMS_DEV)
    dest = jax.vmap(lambda own, number: shared_out(jax.random.fold_in(part_keys[2], 2), own, number, ITEMS_DEV, N_SLAB, 1, CAP, 2))(dest_keys, dest_turns).reshape((ITEMS, 1))
    plane_off = plant(jax.random.randint(part_keys[3], (ITEMS,), 0, ZL), jax.random.fold_in(part_keys[3], 1), 0, ZL - 1).astype(jnp.int32)
    kernel_id = plant(jax.random.randint(part_keys[4], (ITEMS,), 0, NK), jax.random.fold_in(part_keys[4], 1), 0, NK - 1).astype(jnp.int32)
    return {"samples": samples, "kernels": kernels, "dest": dest, "plane_off": plane_off, "kernel_id": kernel_id}


def reverse_bits(values):
    levels = N_SLAB.bit_length() - 1
    total = values * 0
    for level in range(levels):
        total = total + values // 2 ** level % 2 * 2 ** (levels - 1 - level)
    return total

def reference(samples, kernels, dest, plane_off, kernel_id):
    groups = ITEMS // ITEMS_DEV
    planes = (N_SLAB * plane_off + reverse_bits(dest[:, 0])).astype(jnp.int32)
    blocks = (jnp.arange(ITEMS, dtype=jnp.int32) % NB).astype(jnp.int32)

    def add_group(grid, pieces):
        sample_rows, kernel_rows, plane_rows, block_rows = pieces
        tables = kernels[kernel_rows].astype(jnp.float32)
        contrib = jnp.einsum('mrxk,mkj->mxrj', sample_rows.astype(jnp.float32), tables, precision=lax.Precision.HIGHEST)
        grid = grid.at[:, plane_rows, :, block_rows, :].add(contrib)
        return (grid, None)
    start_grid = jnp.zeros((XW, NZ, 2, NB, KW), jnp.float32)
    pieces = (samples.reshape(groups, ITEMS_DEV, 2, XW, KW), kernel_id.reshape(groups, ITEMS_DEV), planes.reshape(groups, ITEMS_DEV), blocks.reshape(groups, ITEMS_DEV))
    grid, unused = lax.scan(add_group, start_grid, pieces)
    grid = grid.reshape(XW, NZ, 2, NY)
    complex_grid = grid[:, :, 0, :] + 1j * grid[:, :, 1, :]
    result = jnp.fft.ifft2(complex_grid, axes=(1, 2)) * math.sqrt(NY * NZ)
    return jnp.stack([jnp.real(result), jnp.imag(result)], axis=0).astype(jnp.float32)
```

```python
import functools
import math

import jax
import jax.numpy as jnp
import numpy as np
from jax import lax
from jax.experimental import pallas as pl
from jax.experimental.pallas import tpu as pltpu
from jax.sharding import PartitionSpec as P

NY = 512
NZ = 512
ROWS = 8
PAIR = 2


def reverse_bits(values, levels):
    total = values * 0
    for level in range(levels):
        total = total + values // 2**level % 2 * 2 ** (levels - 1 - level)
    return total


def y_matrix():
    index = np.arange(NY)
    angle = 2.0 * np.pi / NY * (index[:, None] * index[None, :] % NY)
    c, s = np.cos(angle), np.sin(angle)
    full = np.block([[c, s], [-s, c]]) / math.sqrt(NY * NZ)
    full = full.astype(np.float32)
    high = full.astype(jnp.bfloat16)
    low = (full - high.astype(np.float32)).astype(jnp.bfloat16)
    return high, low


def split(value):
    high = value.astype(jnp.bfloat16)
    low = (value - high.astype(jnp.float32)).astype(jnp.bfloat16)
    return high, low


def chunk_kernel(first, last, y_blocks, z_local, *refs):
    kid_ref, block_ref, table_ref, weight_ref = refs[:4]
    refs = refs[4:]
    if not first:
        before_ref, refs = refs[0], refs[1:]
    if last:
        y_high_ref, y_low_ref = refs[:2]
        out_ref, spread_ref, total_ref = refs[-3:]
    else:
        total_ref, spread_ref = refs
    items, rows, width = block_ref.shape
    per_block = items // y_blocks
    group = 4

    @pl.when(pl.program_id(0) == 0)
    def _():
        def body(step, carry):
            for u in range(group):
                for b in range(y_blocks):
                    q = step * group + u
                    item = q * y_blocks + b
                    value = jnp.dot(
                        block_ref[item],
                        table_ref[kid_ref[item]],
                        preferred_element_type=jnp.float32,
                    )
                    place = pl.multiple_of((b * per_block + q) * rows, rows)
                    spread_ref[pl.ds(place, rows), :] = value
            return carry

        lax.fori_loop(0, per_block // group, body, 0)

    x_first = pl.program_id(0) * PAIR
    for b in range(y_blocks):
        parts = []
        for x in range(PAIR):
            base = b * per_block * rows + x_first + x
            real = spread_ref[pl.ds(base, per_block, stride=rows), :]
            imag = spread_ref[pl.ds(base + rows // 2, per_block, stride=rows), :]
            parts.append(jnp.concatenate([real, imag], axis=0))
        high, low = split(jnp.concatenate(parts, axis=1))
        value = jnp.dot(
            weight_ref[b],
            jnp.concatenate([high, low, high], axis=0),
            preferred_element_type=jnp.float32,
        )
        for x in range(PAIR):
            for part in range(2):
                piece = value[
                    part * z_local : (part + 1) * z_local, x * width : (x + 1) * width
                ]
                at = (
                    slice(x * z_local, (x + 1) * z_local),
                    slice(part * NY + b * width, part * NY + (b + 1) * width),
                )
                if not first:
                    piece = piece + before_ref[at]
                total_ref[at] = piece
    if last:
        high, low = split(total_ref[...])
        for part in range(2):
            columns = slice(part * NY, (part + 1) * NY)
            result = (
                jnp.dot(high, y_high_ref[:, columns], preferred_element_type=jnp.float32)
                + jnp.dot(low, y_high_ref[:, columns], preferred_element_type=jnp.float32)
                + jnp.dot(high, y_low_ref[:, columns], preferred_element_type=jnp.float32)
            )
            for x in range(PAIR):
                out_ref[part, x] = result[x * z_local : (x + 1) * z_local]


def run_chunk(kid, block, table, weight, before, out, y_parts, chunk, last, sizes):
    y_blocks, z_local, x_share = sizes
    items, rows, width = block.shape
    steps = ROWS // PAIR
    first = before is None

    def whole(array):
        zeros = (0,) * array.ndim
        return pl.BlockSpec(array.shape, lambda i: zeros, pipeline_mode=pl.Buffered(1))

    total_spec = pl.BlockSpec((PAIR * z_local, 2 * NY), lambda i: (i, 0))
    args = [kid, block, table, weight]
    specs = [pl.BlockSpec(memory_space=pltpu.SMEM)] + [whole(a) for a in args[1:]]
    if not first:
        args.append(before)
        specs.append(total_spec)
    aliases = {}
    spread = pltpu.VMEM((items * rows, width), jnp.float32)
    if last:
        args += y_parts
        specs += [whole(a) for a in y_parts]
        if out is not None:
            aliases = {len(args): 0}
            args.append(out)
            specs.append(pl.BlockSpec(memory_space=pl.ANY))
        out_shape = jax.ShapeDtypeStruct((2, x_share, z_local, NY), jnp.float32)
        out_spec = pl.BlockSpec(
            (2, PAIR, z_local, NY), lambda i: (0, chunk * steps + i, 0, 0)
        )
        scratch = [spread, pltpu.VMEM((PAIR * z_local, 2 * NY), jnp.float32)]
    else:
        out_shape = jax.ShapeDtypeStruct((ROWS * z_local, 2 * NY), jnp.float32)
        out_spec = total_spec
        scratch = [spread]
    flops = 2 * items * rows * width * width + 2 * 3 * 2 * z_local * 2 * items * ROWS * width
    if last:
        flops += 2 * 3 * ROWS * z_local * 4 * NY * NY
    return pl.pallas_call(
        functools.partial(chunk_kernel, first, last, y_blocks, z_local),
        grid=(steps,),
        in_specs=specs,
        out_specs=out_spec,
        out_shape=out_shape,
        scratch_shapes=scratch,
        input_output_aliases=aliases,
        compiler_params=pltpu.CompilerParams(vmem_limit_bytes=40 * 2**20),
        cost_estimate=pl.CostEstimate(
            flops=flops, bytes_accessed=16 * 2**20, transcendentals=0
        ),
    )(*args)


def per_device(samples, kernels, dest, plane_off, kernel_id):
    n_slab = lax.axis_size("slab")
    n_img = lax.axis_size("img")
    levels = n_slab.bit_length() - 1
    items, _, x_rows, k_width = samples.shape
    y_blocks = NY // k_width
    z_local = NZ // n_slab
    x_share = x_rows // n_img
    chunks = x_share // ROWS
    sizes = (y_blocks, z_local, x_share)
    slab, img = lax.axis_index("slab"), lax.axis_index("img")

    planes = n_slab * plane_off + reverse_bits(dest[:, 0], levels)
    meta = lax.all_gather(jnp.stack([planes, kernel_id], axis=0), ("slab", "img"))
    meta = meta.reshape(n_slab, n_img, 2, items)
    meta = meta[(slab - jnp.arange(n_slab)) % n_slab][:, img ^ jnp.arange(n_img)]
    meta = meta.transpose(0, 2, 1, 3).reshape(n_slab, 2, n_img * items)
    kid = meta[:, 1]
    z_of = meta[:, 0].reshape(n_slab, n_img * items // y_blocks, y_blocks).transpose(0, 2, 1)
    z_out = slab * z_local + jnp.arange(z_local, dtype=jnp.int32)
    turn = z_out[None, None, :, None] * z_of[:, :, None, :] % NZ
    angle = 2.0 * math.pi / NZ * turn.astype(jnp.float32)
    c, s = jnp.cos(angle), jnp.sin(angle)
    weight = jnp.concatenate(
        [jnp.concatenate([c, -s], axis=3), jnp.concatenate([s, c], axis=3)], axis=2
    )
    high = lax.reduce_precision(weight, 8, 7)
    low = (weight - high).astype(jnp.bfloat16)
    high = high.astype(jnp.bfloat16)
    weight = jnp.concatenate([high, high, low], axis=3)
    y_parts = [jnp.asarray(a) for a in y_matrix()]

    def rows_for(owner, chunk):
        piece = lax.dynamic_slice_in_dim(samples, owner * x_share + chunk * ROWS, ROWS, axis=2)
        return piece.reshape(items, 2 * ROWS, k_width)

    ring = [(i, (i + 1) % n_slab) for i in range(n_slab)]
    blocks = []
    for chunk in range(chunks):
        pieces = [rows_for(img, chunk)]
        for k in range(1, n_img):
            pairs = [(i, i ^ k) for i in range(n_img)]
            pieces.append(lax.ppermute(rows_for(img ^ k, chunk), "img", pairs))
        held = [jnp.concatenate(pieces, axis=0)]
        for _ in range(1, n_slab):
            held.append(lax.ppermute(held[-1], "slab", ring))
        blocks.append(held)

    out = None
    for chunk in range(chunks):
        total = None
        for step in range(n_slab):
            last = step == n_slab - 1
            value = run_chunk(
                kid[step], blocks[chunk][step], kernels, weight[step], total, out,
                y_parts, chunk, last, sizes,
            )
            if last:
                out = value
            else:
                total = value
    return out


def solution(mesh):
    in_specs = (
        P(("half", "slab", "img"), None, None, None),
        P(),
        P(("half", "slab", "img"), None),
        P(("half", "slab", "img")),
        P(("half", "slab", "img")),
    )
    out_specs = P(None, ("half", "img"), "slab", None)
    return jax.shard_map(
        per_device, mesh=mesh, in_specs=in_specs, out_specs=out_specs, check_vma=False
    )
```

```python
import functools
import math

import jax
import jax.numpy as jnp
import numpy as np
from jax import lax
from jax.experimental import pallas as pl
from jax.experimental.pallas import tpu as pltpu
from jax.sharding import PartitionSpec as P

NY = 512
NZ = 512
ROWS = 8
PAIR = 2


def reverse_bits(values, levels):
    total = values * 0
    for level in range(levels):
        total = total + values // 2**level % 2 * 2 ** (levels - 1 - level)
    return total


def y_matrix():
    index = np.arange(NY)
    angle = 2.0 * np.pi / NY * (index[:, None] * index[None, :] % NY)
    c, s = np.cos(angle), np.sin(angle)
    full = np.block([[c, s], [-s, c]]) / math.sqrt(NY * NZ)
    full = full.astype(np.float32)
    high = full.astype(jnp.bfloat16)
    low = (full - high.astype(np.float32)).astype(jnp.bfloat16)
    return high, low


def split(value):
    high = value.astype(jnp.bfloat16)
    low = (value - high.astype(jnp.float32)).astype(jnp.bfloat16)
    return high, low


def chunk_kernel(first, last, y_blocks, z_local, *refs):
    kid_ref, own_ref, other_ref, table_ref, weight_ref = refs[:5]
    refs = refs[5:]
    if not first:
        before_ref, refs = refs[0], refs[1:]
    if last:
        y_high_ref, y_low_ref = refs[:2]
        out_ref, spread_ref, total_ref = refs[-3:]
    else:
        total_ref, spread_ref = refs
    own, rows, width = own_ref.shape
    others = other_ref.shape[0]
    per_block = (own + others) // y_blocks
    group = 4

    def spread_items(block_ref, first_item):
        def body(step, carry):
            for u in range(group):
                for b in range(y_blocks):
                    q = step * group + u
                    item = q * y_blocks + b
                    value = jnp.dot(
                        block_ref[item],
                        table_ref[kid_ref[first_item + item]],
                        preferred_element_type=jnp.float32,
                    )
                    place = b * per_block + first_item // y_blocks + q
                    spread_ref[pl.ds(pl.multiple_of(place * rows, rows), rows), :] = value
            return carry

        lax.fori_loop(0, block_ref.shape[0] // (y_blocks * group), body, 0)

    @pl.when(pl.program_id(0) == 0)
    def _():
        spread_items(own_ref, 0)
        spread_items(other_ref, own)

    x_first = pl.program_id(0) * PAIR
    for b in range(y_blocks):
        parts = []
        for x in range(PAIR):
            base = b * per_block * rows + x_first + x
            real = spread_ref[pl.ds(base, per_block, stride=rows), :]
            imag = spread_ref[pl.ds(base + rows // 2, per_block, stride=rows), :]
            parts.append(jnp.concatenate([real, imag], axis=0))
        high, low = split(jnp.concatenate(parts, axis=1))
        value = jnp.dot(
            weight_ref[b],
            jnp.concatenate([high, low, high], axis=0),
            preferred_element_type=jnp.float32,
        )
        for x in range(PAIR):
            for part in range(2):
                piece = value[
                    part * z_local : (part + 1) * z_local, x * width : (x + 1) * width
                ]
                at = (
                    slice(x * z_local, (x + 1) * z_local),
                    slice(part * NY + b * width, part * NY + (b + 1) * width),
                )
                if not first:
                    piece = piece + before_ref[at]
                total_ref[at] = piece
    if last:
        high, low = split(total_ref[...])
        for part in range(2):
            columns = slice(part * NY, (part + 1) * NY)
            result = (
                jnp.dot(high, y_high_ref[:, columns], preferred_element_type=jnp.float32)
                + jnp.dot(low, y_high_ref[:, columns], preferred_element_type=jnp.float32)
                + jnp.dot(high, y_low_ref[:, columns], preferred_element_type=jnp.float32)
            )
            for x in range(PAIR):
                out_ref[part, x] = result[x * z_local : (x + 1) * z_local]


def run_chunk(kid, own, other, table, weight, before, out, y_parts, chunk, last, sizes):
    y_blocks, z_local, x_share = sizes
    rows, width = other.shape[1:]
    items = own.shape[1] + other.shape[0]
    steps = ROWS // PAIR
    first = before is None

    def whole(array):
        zeros = (0,) * array.ndim
        return pl.BlockSpec(array.shape, lambda i: zeros, pipeline_mode=pl.Buffered(1))

    total_spec = pl.BlockSpec((PAIR * z_local, 2 * NY), lambda i: (i, 0))
    args = [kid, own, other, table, weight]
    own_spec = pl.BlockSpec(
        (None, *own.shape[1:]), lambda i: (chunk, 0, 0, 0), pipeline_mode=pl.Buffered(1)
    )
    specs = [pl.BlockSpec(memory_space=pltpu.SMEM), own_spec] + [whole(a) for a in args[2:]]
    if not first:
        args.append(before)
        specs.append(total_spec)
    aliases = {}
    spread = pltpu.VMEM((items * rows, width), jnp.float32)
    if last:
        args += y_parts
        specs += [whole(a) for a in y_parts]
        if out is not None:
            aliases = {len(args): 0}
            args.append(out)
            specs.append(pl.BlockSpec(memory_space=pl.ANY))
        out_shape = jax.ShapeDtypeStruct((2, x_share, z_local, NY), jnp.float32)
        out_spec = pl.BlockSpec(
            (2, PAIR, z_local, NY), lambda i: (0, chunk * steps + i, 0, 0)
        )
        scratch = [spread, pltpu.VMEM((PAIR * z_local, 2 * NY), jnp.float32)]
    else:
        out_shape = jax.ShapeDtypeStruct((ROWS * z_local, 2 * NY), jnp.float32)
        out_spec = total_spec
        scratch = [spread]
    flops = 2 * items * rows * width * width + 2 * 3 * 2 * z_local * 2 * items * ROWS * width
    if last:
        flops += 2 * 3 * ROWS * z_local * 4 * NY * NY
    return pl.pallas_call(
        functools.partial(chunk_kernel, first, last, y_blocks, z_local),
        grid=(steps,),
        in_specs=specs,
        out_specs=out_spec,
        out_shape=out_shape,
        scratch_shapes=scratch,
        input_output_aliases=aliases,
        compiler_params=pltpu.CompilerParams(vmem_limit_bytes=40 * 2**20),
        cost_estimate=pl.CostEstimate(
            flops=flops, bytes_accessed=16 * 2**20, transcendentals=0
        ),
    )(*args)


def per_device(samples, kernels, dest, plane_off, kernel_id):
    n_slab = lax.axis_size("slab")
    n_img = lax.axis_size("img")
    levels = n_slab.bit_length() - 1
    items, _, x_rows, k_width = samples.shape
    y_blocks = NY // k_width
    z_local = NZ // n_slab
    x_share = x_rows // n_img
    chunks = x_share // ROWS
    sizes = (y_blocks, z_local, x_share)
    slab, img = lax.axis_index("slab"), lax.axis_index("img")

    planes = n_slab * plane_off + reverse_bits(dest[:, 0], levels)
    labels = jnp.stack([planes, kernel_id], axis=0)
    ring = [(i, (i + 1) % n_slab) for i in range(n_slab)]

    def shift(array, step):
        return lax.ppermute(array, "slab", [(i, (i + step) % n_slab) for i in range(n_slab)])

    def swap(array, k):
        return lax.ppermute(array, "img", [(i, i ^ k) for i in range(n_img)])

    by_step = jnp.stack([labels] + [shift(labels, t) for t in range(1, n_slab)])
    by_step, samples = lax.optimization_barrier((by_step, samples))
    meta = jnp.stack([by_step] + [swap(by_step, k) for k in range(1, n_img)])
    meta = meta.transpose(1, 2, 0, 3).reshape(n_slab, 2, n_img * items)
    kid = meta[:, 1]
    z_of = meta[:, 0].reshape(n_slab, n_img * items // y_blocks, y_blocks).transpose(0, 2, 1)
    z_out = slab * z_local + jnp.arange(z_local, dtype=jnp.int32)
    turn = z_out[None, None, :, None] * z_of[:, :, None, :] % NZ
    angle = 2.0 * math.pi / NZ * turn.astype(jnp.float32)
    c, s = jnp.cos(angle), jnp.sin(angle)
    weight = jnp.concatenate(
        [jnp.concatenate([c, -s], axis=3), jnp.concatenate([s, c], axis=3)], axis=2
    )
    high = lax.reduce_precision(weight, 8, 7)
    low = (weight - high).astype(jnp.bfloat16)
    high = high.astype(jnp.bfloat16)
    weight = jnp.concatenate([high, high, low], axis=3)
    y_parts = [jnp.asarray(a) for a in y_matrix()]

    by_rows = samples.reshape(items, 2, n_img, chunks, ROWS, k_width).transpose(2, 3, 0, 1, 4, 5)
    by_rows = by_rows.reshape(n_img, chunks, items, 2 * ROWS, k_width)

    def rows_for(owner):
        return lax.dynamic_index_in_dim(by_rows, owner, 0, keepdims=False)

    own = [rows_for(img)]
    sends = [rows_for(img ^ k) for k in range(1, n_img)]
    others = []
    for chunk in range(chunks):
        if chunk > 0:
            sends, others[-1] = lax.optimization_barrier((sends, others[-1]))
        got = [swap(array[chunk], k + 1) for k, array in enumerate(sends)]
        others.append([jnp.concatenate(got, axis=0)])

    streams = [own] + others
    order = sorted(
        (4 * step + max(0, 7 * n - 5), n, step + 1)
        for n in range(chunks + 1)
        for step in range(n_slab - 1)
    )
    place = {(n, step): at for at, (_, n, step) in enumerate(order)}
    total, taken, out = [None] * chunks, [0] * chunks, None

    def work(chunk, out):
        step = taken[chunk]
        value = run_chunk(
            kid[step], own[step], others[chunk][step], kernels, weight[step], total[chunk], out,
            y_parts, chunk, step == n_slab - 1, sizes,
        )
        taken[chunk] = step + 1
        return value

    for at, (_, n, step) in enumerate(order):
        send = streams[n][step - 1]
        if at >= 2:
            _, m, ahead = order[at - 2]
            send, streams[m][ahead] = lax.optimization_barrier((send, streams[m][ahead]))
        for chunk in range(chunks if at >= 3 else 0):
            step_of = taken[chunk]
            if step_of == n_slab or any(
                place.get((k, step_of), 0) > at - 3 for k in (0, chunk + 1)
            ):
                continue
            value = work(chunk, out)
            send, value = lax.optimization_barrier((send, value))
            if taken[chunk] == n_slab:
                out = value
            else:
                total[chunk] = value
            break
        streams[n].append(lax.ppermute(send, "slab", ring))
    for chunk in range(chunks):
        while taken[chunk] < n_slab:
            value = work(chunk, out)
            if taken[chunk] == n_slab:
                out = value
            else:
                total[chunk] = value
    return out


def solution(mesh):
    in_specs = (
        P(("half", "slab", "img"), None, None, None),
        P(),
        P(("half", "slab", "img"), None),
        P(("half", "slab", "img")),
        P(("half", "slab", "img")),
    )
    out_specs = P(None, ("half", "img"), "slab", None)
    return jax.shard_map(
        per_device, mesh=mesh, in_specs=in_specs, out_specs=out_specs, check_vma=False
    )
```

```python
import functools
import math

import jax
import jax.numpy as jnp
import numpy as np
from jax import lax
from jax.experimental import pallas as pl
from jax.experimental.pallas import tpu as pltpu
from jax.sharding import PartitionSpec as P

NY = 512
NZ = 512
ROWS = 8
PAIR = 2


def reverse_bits(values, levels):
    total = values * 0
    for level in range(levels):
        total = total + values // 2**level % 2 * 2 ** (levels - 1 - level)
    return total


def y_matrix():
    index = np.arange(NY)
    angle = 2.0 * np.pi / NY * (index[:, None] * index[None, :] % NY)
    c, s = np.cos(angle), np.sin(angle)
    full = np.block([[c, s], [-s, c]]) / math.sqrt(NY * NZ)
    full = full.astype(np.float32)
    high = full.astype(jnp.bfloat16)
    low = (full - high.astype(np.float32)).astype(jnp.bfloat16)
    return high, low


def split(value):
    high = value.astype(jnp.bfloat16)
    low = (value - high.astype(jnp.float32)).astype(jnp.bfloat16)
    return high, low


def chunk_kernel(first, last, y_blocks, z_local, *refs):
    kid_ref, own_ref, other_ref, table_ref, weight_ref = refs[:5]
    refs = refs[5:]
    if not first:
        before_ref, refs = refs[0], refs[1:]
    if last:
        y_high_ref, y_low_ref = refs[:2]
        out_ref, spread_ref, total_ref = refs[-3:]
    else:
        total_ref, spread_ref = refs
    own, rows, width = own_ref.shape
    others = other_ref.shape[0]
    per_block = (own + others) // y_blocks
    group = 4

    def spread_items(block_ref, first_item):
        def body(step, carry):
            for u in range(group):
                for b in range(y_blocks):
                    q = step * group + u
                    item = q * y_blocks + b
                    value = jnp.dot(
                        block_ref[item],
                        table_ref[kid_ref[first_item + item]],
                        preferred_element_type=jnp.float32,
                    )
                    place = b * per_block + first_item // y_blocks + q
                    spread_ref[pl.ds(pl.multiple_of(place * rows, rows), rows), :] = value
            return carry

        lax.fori_loop(0, block_ref.shape[0] // (y_blocks * group), body, 0)

    @pl.when(pl.program_id(0) == 0)
    def _():
        spread_items(own_ref, 0)
        spread_items(other_ref, own)

    x_first = pl.program_id(0) * PAIR
    for b in range(y_blocks):
        parts = []
        for x in range(PAIR):
            base = b * per_block * rows + x_first + x
            real = spread_ref[pl.ds(base, per_block, stride=rows), :]
            imag = spread_ref[pl.ds(base + rows // 2, per_block, stride=rows), :]
            parts.append(jnp.concatenate([real, imag], axis=0))
        high, low = split(jnp.concatenate(parts, axis=1))
        value = jnp.dot(
            weight_ref[b],
            jnp.concatenate([high, low, high], axis=0),
            preferred_element_type=jnp.float32,
        )
        for x in range(PAIR):
            for part in range(2):
                piece = value[
                    part * z_local : (part + 1) * z_local, x * width : (x + 1) * width
                ]
                at = (
                    slice(x * z_local, (x + 1) * z_local),
                    slice(part * NY + b * width, part * NY + (b + 1) * width),
                )
                if not first:
                    piece = piece + before_ref[at]
                total_ref[at] = piece
    if last:
        high, low = split(total_ref[...])
        for part in range(2):
            columns = slice(part * NY, (part + 1) * NY)
            result = (
                jnp.dot(high, y_high_ref[:, columns], preferred_element_type=jnp.float32)
                + jnp.dot(low, y_high_ref[:, columns], preferred_element_type=jnp.float32)
                + jnp.dot(high, y_low_ref[:, columns], preferred_element_type=jnp.float32)
            )
            for x in range(PAIR):
                out_ref[part, x] = result[x * z_local : (x + 1) * z_local]


def run_chunk(kid, own, other, table, weight, before, out, y_parts, chunk, last, sizes):
    y_blocks, z_local, x_share = sizes
    rows, width = other.shape[1:]
    items = own.shape[1] + other.shape[0]
    steps = ROWS // PAIR
    first = before is None

    def whole(array):
        zeros = (0,) * array.ndim
        return pl.BlockSpec(array.shape, lambda i: zeros, pipeline_mode=pl.Buffered(1))

    total_spec = pl.BlockSpec((PAIR * z_local, 2 * NY), lambda i: (i, 0))
    args = [kid, own, other, table, weight]
    own_spec = pl.BlockSpec(
        (None, *own.shape[1:]), lambda i: (chunk, 0, 0, 0), pipeline_mode=pl.Buffered(1)
    )
    specs = [pl.BlockSpec(memory_space=pltpu.SMEM), own_spec] + [whole(a) for a in args[2:]]
    if not first:
        args.append(before)
        specs.append(total_spec)
    aliases = {}
    spread = pltpu.VMEM((items * rows, width), jnp.float32)
    if last:
        args += y_parts
        specs += [whole(a) for a in y_parts]
        if out is not None:
            aliases = {len(args): 0}
            args.append(out)
            specs.append(pl.BlockSpec(memory_space=pl.ANY))
        out_shape = jax.ShapeDtypeStruct((2, x_share, z_local, NY), jnp.float32)
        out_spec = pl.BlockSpec(
            (2, PAIR, z_local, NY), lambda i: (0, chunk * steps + i, 0, 0)
        )
        scratch = [spread, pltpu.VMEM((PAIR * z_local, 2 * NY), jnp.float32)]
    else:
        out_shape = jax.ShapeDtypeStruct((ROWS * z_local, 2 * NY), jnp.float32)
        out_spec = total_spec
        scratch = [spread]
    flops = 2 * items * rows * width * width + 2 * 3 * 2 * z_local * 2 * items * ROWS * width
    if last:
        flops += 2 * 3 * ROWS * z_local * 4 * NY * NY
    return pl.pallas_call(
        functools.partial(chunk_kernel, first, last, y_blocks, z_local),
        grid=(steps,),
        in_specs=specs,
        out_specs=out_spec,
        out_shape=out_shape,
        scratch_shapes=scratch,
        input_output_aliases=aliases,
        compiler_params=pltpu.CompilerParams(vmem_limit_bytes=40 * 2**20),
        cost_estimate=pl.CostEstimate(
            flops=flops, bytes_accessed=16 * 2**20, transcendentals=0
        ),
    )(*args)


def per_device(samples, kernels, dest, plane_off, kernel_id):
    n_slab = lax.axis_size("slab")
    n_img = lax.axis_size("img")
    levels = n_slab.bit_length() - 1
    items, _, x_rows, k_width = samples.shape
    y_blocks = NY // k_width
    z_local = NZ // n_slab
    x_share = x_rows // n_img
    chunks = x_share // ROWS
    sizes = (y_blocks, z_local, x_share)
    slab, img = lax.axis_index("slab"), lax.axis_index("img")

    planes = n_slab * plane_off + reverse_bits(dest[:, 0], levels)
    labels = jnp.stack([planes, kernel_id], axis=0)
    ring = [(i, (i + 1) % n_slab) for i in range(n_slab)]

    def shift(array, step):
        return lax.ppermute(array, "slab", [(i, (i + step) % n_slab) for i in range(n_slab)])

    def swap(array, k):
        return lax.ppermute(array, "img", [(i, i ^ k) for i in range(n_img)])

    by_step = jnp.stack([labels] + [shift(labels, t) for t in range(1, n_slab)])
    by_step, samples = lax.optimization_barrier((by_step, samples))
    meta = jnp.stack([by_step] + [swap(by_step, k) for k in range(1, n_img)])
    meta = meta.transpose(1, 2, 0, 3).reshape(n_slab, 2, n_img * items)
    kid = meta[:, 1]
    z_of = meta[:, 0].reshape(n_slab, n_img * items // y_blocks, y_blocks).transpose(0, 2, 1)
    z_out = slab * z_local + jnp.arange(z_local, dtype=jnp.int32)
    turn = z_out[None, None, :, None] * z_of[:, :, None, :] % NZ
    angle = 2.0 * math.pi / NZ * turn.astype(jnp.float32)
    c, s = jnp.cos(angle), jnp.sin(angle)
    weight = jnp.concatenate(
        [jnp.concatenate([c, -s], axis=3), jnp.concatenate([s, c], axis=3)], axis=2
    )
    high = lax.reduce_precision(weight, 8, 7)
    low = (weight - high).astype(jnp.bfloat16)
    high = high.astype(jnp.bfloat16)
    weight = jnp.concatenate([high, high, low], axis=3)
    y_parts = [jnp.asarray(a) for a in y_matrix()]

    by_rows = samples.reshape(items, 2, n_img, chunks, ROWS, k_width).transpose(2, 3, 0, 1, 4, 5)
    by_rows = by_rows.reshape(n_img, chunks, items, 2 * ROWS, k_width)

    def rows_for(owner):
        return lax.dynamic_index_in_dim(by_rows, owner, 0, keepdims=False)

    own = [rows_for(img)]
    sends = [rows_for(img ^ k) for k in range(1, n_img)]
    others = []
    for chunk in range(chunks):
        if chunk > 0:
            sends, others[-1] = lax.optimization_barrier((sends, others[-1]))
        got = [swap(array[chunk], k + 1) for k, array in enumerate(sends)]
        others.append([jnp.concatenate(got, axis=0)])

    streams = [own] + others
    order = sorted(
        (4 * step + max(0, 7 * n - 5), n, step + 1)
        for n in range(chunks + 1)
        for step in range(n_slab - 1)
    )
    place = {(n, step): at for at, (_, n, step) in enumerate(order)}
    total, taken, out = [None] * chunks, [0] * chunks, None

    def work(chunk, out):
        step = taken[chunk]
        value = run_chunk(
            kid[step], own[step], others[chunk][step], kernels, weight[step], total[chunk], out,
            y_parts, chunk, step == n_slab - 1, sizes,
        )
        taken[chunk] = step + 1
        return value

    for at, (_, n, step) in enumerate(order):
        send = streams[n][step - 1]
        if at >= 2:
            _, m, ahead = order[at - 2]
            send, streams[m][ahead] = lax.optimization_barrier((send, streams[m][ahead]))
        for chunk in range(chunks if at >= 3 else 0):
            final = at == len(order) - 1
            step_of = taken[chunk]
            if step_of == n_slab or any(
                place.get((k, step_of), 0) > at - (2 if final else 3) for k in (0, chunk + 1)
            ):
                continue
            value = work(chunk, out)
            send, value = lax.optimization_barrier((send, value))
            if taken[chunk] == n_slab:
                out = value
            else:
                total[chunk] = value
            if not final:
                break
        streams[n].append(lax.ppermute(send, "slab", ring))
    for chunk in range(chunks):
        while taken[chunk] < n_slab:
            value = work(chunk, out)
            if taken[chunk] == n_slab:
                out = value
            else:
                total[chunk] = value
    return out


def solution(mesh):
    in_specs = (
        P(("half", "slab", "img"), None, None, None),
        P(),
        P(("half", "slab", "img"), None),
        P(("half", "slab", "img")),
        P(("half", "slab", "img")),
    )
    out_specs = P(None, ("half", "img"), "slab", None)
    return jax.shard_map(
        per_device, mesh=mesh, in_specs=in_specs, out_specs=out_specs, check_vma=False
    )
```
